32 devices in a mesh: row: 4 (over y, core), col: 8 (over z, x).
Axes of the slice: x: 2, y: 2, z: 4, core: 2. Of those that a mesh axis runs over, the one named last changes fastest.
Arguments:
- points: float32 [4, 4, 256, 128], P(None, 'row'), may hold values from -1 to 1
- rhs: float32 [4, 4, 256, 256], P(None, 'row', None, 'col'), may hold values from -6 to 6
Outputs:
- factored: float32 [4, 4, 256, 2, 8, 256], P(None, 'row', None, None, 'col')
- solved: float32 [4, 4, 256, 256], P(None, 'row', None, 'col')
The draws below stay inside these ranges and needn't reach their ends.
All inputs are finite; a program needn't handle non-finite values.
Results may differ from the reference program's by a relative error of at most 0.0003.
Values sent between devices are 32-bit elements; how exact they have to be, the bound alone decides.
A program may use at most 64 MiB of HBM per device.

```python
import jax
import jax.numpy as jnp
from jax import lax

F = 128
B = 256
NRHS = 256
PANELS = 2
NT = 16
N_ROW = 4
N_COL = 8


def block_levels(own_key, extent, pieces, least, largest):
    def one(dim, parts):
        heights = jax.random.uniform(jax.random.fold_in(jax.random.fold_in(own_key, 6), dim), (parts,), jnp.float32, least / len(pieces), largest / len(pieces))
        return jnp.repeat(jnp.exp(heights), extent[dim] // parts).reshape((-1,) + (1,) * (len(extent) - dim - 1))

    factor_of = one(*pieces[0])
    for cut in pieces[1:]:
        factor_of = factor_of * one(*cut)
    return factor_of


def centred(own_key, shape, width, bound, pieces=(), kind=jnp.bfloat16):
    values = width * jax.random.normal(own_key, shape, jnp.float32)
    if pieces:
        values = values * block_levels(own_key, shape, pieces, -0.22, 0.18)
    return jnp.clip(values, -bound, bound).astype(kind)


def setup_inputs(seed: int = 0) -> dict:
    key_list = jax.random.split(jax.random.key(seed), 3)
    return {
        "points": jnp.clip(jax.random.uniform(key_list[0], (NT // N_ROW, N_ROW, B, F), jnp.float32, -1.0, 1.0) * block_levels(key_list[0], (NT // N_ROW, N_ROW, B, F), ((1, 4),), -0.4, 0.0), -1.0, 1.0),
        "rhs": centred(key_list[1], (NT // N_ROW, N_ROW, B, NRHS), 1.0, 6.0, ((1, 4), (3, 8)), jnp.float32),
    }


SCALE = 3.0
NUGGET = 1.0
HIGHEST = lax.Precision.HIGHEST

def reference(points, rhs):
    tile_count = points.shape[0] * points.shape[1]
    tile_size = points.shape[2]
    feature_dim = points.shape[3]
    size = tile_count * tile_size
    design = points.reshape(size, feature_dim)
    right_side = rhs.reshape(size, rhs.shape[-1])
    squares = jnp.sum(design * design, axis=1)
    position = jnp.arange(size, dtype=jnp.int32)

    def build_rows(offset):
        segment = lax.dynamic_slice_in_dim(design, offset, tile_size, 0)
        segment_sq = lax.dynamic_slice_in_dim(squares, offset, tile_size, 0)
        inner_prod = jnp.dot(segment, design.T, precision=HIGHEST)
        distance = segment_sq[:, None] + squares[None, :] - 2.0 * inner_prod
        diagonal_hit = ((offset + jnp.arange(tile_size, dtype=jnp.int32))[:, None] == position[None, :]).astype(jnp.float32)
        return jnp.exp(-SCALE / feature_dim * distance) + NUGGET * diagonal_hit
    kernel = lax.map(build_rows, jnp.arange(tile_count, dtype=jnp.int32) * tile_size).reshape(size, size)
    panels = []
    factors = []
    for which_panel in range(PANELS):
        first_row = which_panel * tile_size
        column = kernel[:, first_row:first_row + tile_size]
        for earlier in panels:
            column = column - jnp.dot(earlier, earlier[first_row:first_row + tile_size].T, precision=HIGHEST)
        factor = jnp.linalg.cholesky(column[first_row:first_row + tile_size])
        panel_tile = jax.scipy.linalg.solve_triangular(factor, column.T, lower=True).T
        beneath = (position >= first_row + tile_size)[:, None]
        panel_tile = jnp.where(beneath, panel_tile, 0.0)
        panel_tile = panel_tile.at[first_row:first_row + tile_size].set(factor)
        panels.append(panel_tile)
        factors.append(factor)
    border = PANELS * tile_size
    joined = jnp.concatenate(panels, axis=1)
    trailing = joined[border:]
    schur = kernel[border:, border:] - jnp.dot(trailing, trailing.T, precision=HIGHEST)
    upper_half = jnp.concatenate([joined[:border], jnp.zeros((border, size - border), jnp.float32)], axis=1)
    lower_half = jnp.concatenate([trailing, schur], axis=1)
    factored = jnp.concatenate([upper_half, lower_half], axis=0).reshape(points.shape[0], points.shape[1], tile_size, tile_count // N_COL, N_COL, tile_size)
    answers = []
    for which_panel in range(PANELS):
        first_row = which_panel * tile_size
        segment = right_side[first_row:first_row + tile_size]
        for earlier, answer in zip(panels, answers):
            segment = segment - jnp.dot(earlier[first_row:first_row + tile_size], answer, precision=HIGHEST)
        answers.append(jax.scipy.linalg.solve_triangular(factors[which_panel], segment, lower=True))
    remainder = right_side[border:] - jnp.dot(trailing, jnp.concatenate(answers, axis=0), precision=HIGHEST)
    solved = jnp.concatenate(answers + [remainder], axis=0).reshape(rhs.shape)
    return (factored, solved)
```

```python
import functools

import jax
import jax.numpy as jnp
from jax import lax
from jax.experimental import pallas as pl
from jax.experimental.pallas import tpu as pltpu
from jax.sharding import PartitionSpec as P

PANELS = 2
SCALE = 3.0
NUGGET = 1.0
HIGHEST = lax.Precision.HIGHEST
MESH = pl.DeviceIdType.MESH
F32 = jnp.float32
BF16 = jnp.bfloat16
NB = 64


def fetch_kernel(rows_n, cols_n, tile_cols, pts, prhs, piv, colp, rpiv, send, recv, local):
    row_id = lax.axis_index("row")
    col_id = lax.axis_index("col")
    stride = cols_n // rows_n

    barrier = pltpu.get_barrier_semaphore()
    for step in range(1, rows_n):
        other = lax.rem(row_id + step, rows_n)
        pl.semaphore_signal(barrier, inc=1, device_id={"row": other}, device_id_type=MESH)
    pl.semaphore_wait(barrier, rows_n - 1)

    jobs = []
    for k in range(PANELS):
        jobs.append((k % rows_n, pts.at[k // rows_n], piv.at[k]))
        jobs.append((k % rows_n, prhs.at[k // rows_n], rpiv.at[k]))
    for c2 in range(tile_cols):
        slot = c2 * stride + col_id // rows_n
        jobs.append((lax.rem(col_id, rows_n), pts.at[slot], colp.at[c2]))

    def remote(number, step):
        _, src, dst = jobs[number]
        return pltpu.make_async_remote_copy(
            src_ref=src,
            dst_ref=dst,
            send_sem=send.at[number, step - 1],
            recv_sem=recv.at[number],
            device_id={"row": lax.rem(row_id + step, rows_n)},
            device_id_type=MESH,
        )

    for number, (owner, src, dst) in enumerate(jobs):

        @pl.when(row_id == owner)
        def _(number=number, src=src, dst=dst):
            for step in range(1, rows_n):
                remote(number, step).start()
            pltpu.make_async_copy(src, dst, local.at[number]).start()

    for number, (owner, src, dst) in enumerate(jobs):

        @pl.when(row_id == owner)
        def _(number=number, src=src, dst=dst):
            for step in range(1, rows_n):
                remote(number, step).wait_send()
            pltpu.make_async_copy(src, dst, local.at[number]).wait()

        @pl.when(row_id != owner)
        def _(number=number):
            remote(number, 1).wait_recv()


def split(x):
    hi = x.astype(BF16)
    return hi, (x - hi.astype(F32)).astype(BF16)


def nt(a, b):
    return lax.dot_general(a, b, (((1,), (1,)), ((), ())), preferred_element_type=F32)


def nt3(a, b):
    return nt(a[0], b[0]) + (nt(a[0], b[1]) + nt(a[1], b[0]))


def squared_exp(a, b, b_sq):
    a_sq = jnp.sum(a * a, axis=1, keepdims=True)
    inner = nt3(split(a), split(b))
    return jnp.exp((-SCALE / a.shape[1]) * (a_sq + b_sq - 2.0 * inner))


def row_squares(b):
    ones = jnp.ones((8, b.shape[1]), F32)
    return lax.dot_general(
        ones, b * b, (((1,), (1,)), ((), ())), precision=HIGHEST, preferred_element_type=F32
    )[:1]


def base_inverse(block):
    lane = lax.broadcasted_iota(jnp.int32, (8, 2 * NB), 1)
    sub = lax.broadcasted_iota(jnp.int32, (8, 2 * NB), 0)
    eye = (
        lax.broadcasted_iota(jnp.int32, (NB, NB), 0) == lax.broadcasted_iota(jnp.int32, (NB, NB), 1)
    ).astype(F32)
    wide = jnp.concatenate([block, eye], axis=1)
    v = [wide[8 * q : 8 * q + 8] for q in range(NB // 8)]
    for j in range(NB):
        q0, s = divmod(j, 8)
        row = v[q0][s : s + 1]
        scaled = row * (1.0 / row[:, j : j + 1])
        for q in range(q0, NB // 8):
            col = v[q][:, j : j + 1]
            if q == q0:
                if s == 7:
                    continue
                col = jnp.where(sub[:, :1] > s, col, 0.0)
            v[q] = v[q] - col * scaled
    out = []
    for q in range(NB // 8):
        diag = jnp.sum(jnp.where(lane == sub + 8 * q, v[q], 0.0), axis=1, keepdims=True)
        out.append(v[q] * lax.rsqrt(diag))
    return jnp.concatenate(out, axis=0)[:, NB:]


def inverse_factor(w, h):
    size = h.shape[0]
    for j0 in range(0, size, NB):
        j1 = j0 + NB
        inv = base_inverse(w[j0:j1, j0:j1])
        rows = jnp.dot(inv, w[j0:j1, :], precision=HIGHEST, preferred_element_type=F32)
        h[j0:j1, :] = rows[:, size:]
        if j1 < size:
            panel = lax.dot_general(
                w[j1:, j0:j1], inv, (((1,), (1,)), ((), ())), precision=HIGHEST, preferred_element_type=F32
            )
            w[j1:, :] = w[j1:, :] - jnp.dot(
                panel, rows, precision=HIGHEST, preferred_element_type=F32
            )


def main_kernel(
    rows_n, cols_n, pts, piv, colp, rhs, rpiv, out, solved, w, h0, h1, l10, lf, lh, ll, yh, yl
):
    row_id = lax.axis_index("row")
    col_id = lax.axis_index("col")
    tile_rows, size, _ = pts.shape
    tile_cols = colp.shape[0]
    row_in = lax.broadcasted_iota(jnp.int32, (size, size), 0)
    col_in = lax.broadcasted_iota(jnp.int32, (size, size), 1)
    eye = (row_in == col_in).astype(F32)
    lower = row_in >= col_in
    x0, x1 = piv[0], piv[1]
    sq0, sq1 = row_squares(x0), row_squares(x1)

    w[:, :size] = squared_exp(x0, x0, sq0) + NUGGET * eye
    w[:, size:] = eye
    inverse_factor(w, h0)
    h0s = split(h0[...])
    l10[...] = nt3(split(squared_exp(x1, x0, sq0)), h0s)
    l10s = split(l10[...])
    w[:, :size] = squared_exp(x1, x1, sq1) + NUGGET * eye - nt3(l10s, l10s)
    w[:, size:] = eye
    inverse_factor(w, h1)
    h1s = split(h1[...])

    y0 = nt3(split(rpiv[0]), h0s)
    y1 = nt3(split(rpiv[1] - nt3(split(y0), l10s)), h1s)
    yh[:, :size], yl[:, :size] = split(y0)
    yh[:, size:], yl[:, size:] = split(y1)

    def panels_of(x, tile):
        k0 = squared_exp(x, x0, sq0) + jnp.where(tile == 0, NUGGET, 0.0) * eye
        l0 = nt3(split(k0), h0s)
        l0 = jnp.where((tile != 0) | lower, l0, 0.0)
        k1 = squared_exp(x, x1, sq1) + jnp.where(tile == 1, NUGGET, 0.0) * eye
        l1 = nt3(split(k1 - nt3(split(l0), l10s)), h1s)
        l1 = jnp.where((tile > 1) | (lower & (tile == 1)), l1, 0.0)
        return l0, l1

    @pl.loop(0, tile_cols)
    def _(c2):
        l0, l1 = panels_of(colp[c2], c2 * cols_n + col_id)
        lh[c2, :, :size], ll[c2, :, :size] = split(l0)
        lh[c2, :, size:], ll[c2, :, size:] = split(l1)

    @pl.loop(0, tile_rows)
    def _(a):
        tile = a * rows_n + row_id
        x = pts[a]
        l0, l1 = panels_of(x, tile)
        lf[:, :size] = l0
        lf[:, size:] = l1
        ls = split(lf[...])
        rest = rhs[a] - nt3((yh[...], yl[...]), ls)
        solved[a] = jnp.where(tile == 0, y0, jnp.where(tile == 1, y1, rest))
        for c2 in range(tile_cols):
            tile_c = c2 * cols_n + col_id
            xc = colp[c2]
            k = squared_exp(x, xc, row_squares(xc)) + jnp.where(tile == tile_c, NUGGET, 0.0) * eye
            s = k - nt3(ls, (lh[c2], ll[c2]))
            s = jnp.where(tile >= PANELS, s, 0.0)
            if c2 == 0:
                s = jnp.where(tile_c == 0, lf[:, :size], jnp.where(tile_c == 1, lf[:, size:], s))
            for half in range(size // 128):
                out[a, pl.ds(c2 * (size // 128) + half, size, stride=tile_cols * size // 128), :] = s[
                    :, half * 128 : half * 128 + 128
                ]


def per_device(points, rhs):
    rows_n = lax.axis_size("row")
    cols_n = lax.axis_size("col")
    tile_rows, _, size, feat = points.shape
    width = rhs.shape[-1]
    tile_cols = tile_rows * rows_n // cols_n
    pts = points[:, 0]
    right = rhs[:, 0].swapaxes(1, 2)
    jobs = 2 * PANELS + tile_cols
    any_spec = pl.BlockSpec(memory_space=pl.ANY)
    vmem = pl.BlockSpec(memory_space=pltpu.VMEM)
    piv, colp, rpiv = pl.pallas_call(
        functools.partial(fetch_kernel, rows_n, cols_n, tile_cols),
        out_shape=(
            jax.ShapeDtypeStruct((PANELS, size, feat), F32),
            jax.ShapeDtypeStruct((tile_cols, size, feat), F32),
            jax.ShapeDtypeStruct((PANELS, width, size), F32),
        ),
        in_specs=[any_spec] * 2,
        out_specs=(any_spec,) * 3,
        scratch_shapes=[
            pltpu.SemaphoreType.DMA((jobs, rows_n - 1)),
            pltpu.SemaphoreType.DMA((jobs,)),
            pltpu.SemaphoreType.DMA((jobs,)),
        ],
        compiler_params=pltpu.CompilerParams(collective_id=0, has_side_effects=True),
        name="fetch",
    )(pts, right)
    factored, solved = pl.pallas_call(
        functools.partial(main_kernel, rows_n, cols_n),
        out_shape=(
            jax.ShapeDtypeStruct((tile_rows, size * tile_cols * size // 128, 128), F32),
            jax.ShapeDtypeStruct((tile_rows, width, size), F32),
        ),
        in_specs=[vmem] * 5,
        out_specs=(vmem,) * 2,
        scratch_shapes=[
            pltpu.VMEM((size, 2 * size), F32),
            pltpu.VMEM((size, size), F32),
            pltpu.VMEM((size, size), F32),
            pltpu.VMEM((size, size), F32),
            pltpu.VMEM((size, 2 * size), F32),
            pltpu.VMEM((tile_cols, size, 2 * size), BF16),
            pltpu.VMEM((tile_cols, size, 2 * size), BF16),
            pltpu.VMEM((width, 2 * size), BF16),
            pltpu.VMEM((width, 2 * size), BF16),
        ],
        compiler_params=pltpu.CompilerParams(vmem_limit_bytes=48 * 1024 * 1024),
        name="panels",
    )(pts, piv, colp, right, rpiv)
    factored = factored.reshape(tile_rows, 1, size, tile_cols, 1, size)
    return factored, solved.swapaxes(1, 2)[:, None]


def solution(mesh):
    return jax.shard_map(
        per_device,
        mesh=mesh,
        in_specs=(P(None, "row", None, None), P(None, "row", None, "col")),
        out_specs=(P(None, "row", None, None, "col", None), P(None, "row", None, "col")),
        check_vma=False,
    )
```

```python
import functools

import jax
import jax.numpy as jnp
from jax import lax
from jax.experimental import pallas as pl
from jax.experimental.pallas import tpu as pltpu
from jax.sharding import PartitionSpec as P

PANELS = 2
SCALE = 3.0
NUGGET = 1.0
HIGHEST = lax.Precision.HIGHEST
MESH = pl.DeviceIdType.MESH
F32 = jnp.float32
BF16 = jnp.bfloat16
NB = 64


def fetch_kernel(rows_n, cols_n, tile_cols, pts, prhs, piv, colp, rpiv, send, recv, local):
    row_id = lax.axis_index("row")
    col_id = lax.axis_index("col")
    stride = cols_n // rows_n

    barrier = pltpu.get_barrier_semaphore()
    for step in range(1, rows_n):
        other = lax.rem(row_id + step, rows_n)
        pl.semaphore_signal(barrier, inc=1, device_id={"row": other}, device_id_type=MESH)
    pl.semaphore_wait(barrier, rows_n - 1)

    jobs = []
    for k in range(PANELS):
        jobs.append((k % rows_n, pts.at[k // rows_n], piv.at[k]))
        jobs.append((k % rows_n, prhs.at[k // rows_n], rpiv.at[k]))
    for c2 in range(tile_cols):
        slot = c2 * stride + col_id // rows_n
        jobs.append((lax.rem(col_id, rows_n), pts.at[slot], colp.at[c2]))

    chips = rows_n // 2
    chip, core = row_id // 2, lax.rem(row_id, 2)
    sibling = row_id + 1 - 2 * core

    def half_of(ref, half):
        height = ref.shape[0] // 2
        return ref.at[pl.ds(pl.multiple_of(half * height, height), height)]

    def remote(number, half, dest, slot, relay=False):
        _, src, dst = jobs[number]
        return pltpu.make_async_remote_copy(
            src_ref=half_of(dst if relay else src, half),
            dst_ref=half_of(dst, half),
            send_sem=send.at[number, slot],
            recv_sem=recv.at[number, half],
            device_id={"row": dest},
            device_id_type=MESH,
        )

    def sends(number):
        out = []
        for step in range(1, chips):
            for half in range(2):
                dest = 2 * lax.rem(chip + step, chips) + half
                out.append(remote(number, half, dest, 2 * step + half))
        return out + [remote(number, half, sibling, half) for half in range(2)]

    for number, (owner, src, dst) in enumerate(jobs):

        @pl.when(row_id == owner)
        def _(number=number, src=src, dst=dst):
            for copy in sends(number):
                copy.start()
            pltpu.make_async_copy(src, dst, local.at[number]).start()

    for number, (owner, src, dst) in enumerate(jobs):

        @pl.when(chip != owner // 2)
        def _(number=number):
            relay = remote(number, core, sibling, 0, relay=True)
            relay.wait_recv()
            relay.start()

    for number, (owner, src, dst) in enumerate(jobs):

        @pl.when(row_id == owner)
        def _(number=number, src=src, dst=dst):
            for copy in sends(number):
                copy.wait_send()
            pltpu.make_async_copy(src, dst, local.at[number]).wait()

        @pl.when(sibling == owner)
        def _(number=number):
            for half in range(2):
                remote(number, half, sibling, half).wait_recv()

        @pl.when(chip != owner // 2)
        def _(number=number):
            remote(number, core, sibling, 0, relay=True).wait_send()
            remote(number, 1 - core, sibling, 0, relay=True).wait_recv()


def split(x):
    hi = x.astype(BF16)
    return hi, (x - hi.astype(F32)).astype(BF16)


def nt(a, b):
    return lax.dot_general(a, b, (((1,), (1,)), ((), ())), preferred_element_type=F32)


def nt3(a, b):
    return nt(a[0], b[0]) + (nt(a[0], b[1]) + nt(a[1], b[0]))


def squared_exp(a, b, b_sq):
    a_sq = jnp.sum(a * a, axis=1, keepdims=True)
    inner = nt3(split(a), split(b))
    return jnp.exp((-SCALE / a.shape[1]) * (a_sq + b_sq - 2.0 * inner))


def row_squares(b):
    ones = jnp.ones((8, b.shape[1]), F32)
    return lax.dot_general(
        ones, b * b, (((1,), (1,)), ((), ())), precision=HIGHEST, preferred_element_type=F32
    )[:1]


def base_inverse(block, base):
    eye = (
        lax.broadcasted_iota(jnp.int32, (NB, NB), 0) == lax.broadcasted_iota(jnp.int32, (NB, NB), 1)
    ).astype(F32)
    wide = jnp.concatenate([block, eye], axis=1)
    v = [wide[8 * q : 8 * q + 8] for q in range(NB // 8)]
    for j in range(0, NB, 2):
        q0, s = divmod(j, 8)
        r0, r1 = v[q0][s : s + 1], v[q0][s + 1 : s + 2]
        a, b = r0[:, j : j + 1], r0[:, j + 1 : j + 2]
        b1, c = r1[:, j : j + 1], r1[:, j + 1 : j + 2]
        det = a * c - b * b1
        inv_det = 1.0 / det
        s0 = (c * r0 - b * r1) * inv_det
        s1 = (a * r1 - b1 * r0) * inv_det
        rs = lax.rsqrt(a)
        base[j : j + 1, :] = r0 * rs
        base[j + 1 : j + 2, :] = (a * r1 - b1 * r0) * (lax.rsqrt(det) * rs)
        for q in range(q0 if s < 6 else q0 + 1, NB // 8):
            v[q] = v[q] - v[q][:, j : j + 1] * s0 - v[q][:, j + 1 : j + 2] * s1
    return base[:, NB:]


def inverse_factor(w, h, base):
    size = h.shape[0]
    for j0 in range(0, size, NB):
        j1 = j0 + NB
        inv = base_inverse(w[j0:j1, j0:j1], base)
        rows = jnp.dot(inv, w[j0:j1, :], precision=HIGHEST, preferred_element_type=F32)
        h[j0:j1, :] = rows[:, size:]
        if j1 < size:
            panel = lax.dot_general(
                w[j1:, j0:j1], inv, (((1,), (1,)), ((), ())), precision=HIGHEST, preferred_element_type=F32
            )
            w[j1:, :] = w[j1:, :] - jnp.dot(
                panel, rows, precision=HIGHEST, preferred_element_type=F32
            )


def main_kernel(
    rows_n, cols_n, hpts, hpiv, hcolp, hrhs, hrpiv, out, solved,
    pts, piv, colp, rhs, rpiv, sems, base, w, h0, h1, l10, lf, lh, ll, yh, yl,
):
    copies = [
        pltpu.make_async_copy(src, dst, sems.at[n])
        for n, (src, dst) in enumerate(
            ((hpiv, piv), (hrpiv, rpiv), (hcolp, colp), (hpts, pts), (hrhs, rhs))
        )
    ]
    for copy in copies:
        copy.start()
    copies[0].wait()
    row_id = lax.axis_index("row")
    col_id = lax.axis_index("col")
    tile_rows, size, _ = pts.shape
    tile_cols = colp.shape[0]
    row_in = lax.broadcasted_iota(jnp.int32, (size, size), 0)
    col_in = lax.broadcasted_iota(jnp.int32, (size, size), 1)
    eye = (row_in == col_in).astype(F32)
    lower = row_in >= col_in
    x0, x1 = piv[0], piv[1]
    sq0, sq1 = row_squares(x0), row_squares(x1)

    w[:, :size] = squared_exp(x0, x0, sq0) + NUGGET * eye
    w[:, size:] = eye
    inverse_factor(w, h0, base)
    h0s = split(h0[...])
    l10[...] = nt3(split(squared_exp(x1, x0, sq0)), h0s)
    l10s = split(l10[...])
    w[:, :size] = squared_exp(x1, x1, sq1) + NUGGET * eye - nt3(l10s, l10s)
    w[:, size:] = eye
    inverse_factor(w, h1, base)
    h1s = split(h1[...])

    for copy in copies[1:]:
        copy.wait()
    y0 = nt3(split(rpiv[0]), h0s)
    y1 = nt3(split(rpiv[1] - nt3(split(y0), l10s)), h1s)
    yh[:, :size], yl[:, :size] = split(y0)
    yh[:, size:], yl[:, size:] = split(y1)

    def panels_of(x, tile):
        k0 = squared_exp(x, x0, sq0) + jnp.where(tile == 0, NUGGET, 0.0) * eye
        l0 = nt3(split(k0), h0s)
        l0 = jnp.where((tile != 0) | lower, l0, 0.0)
        k1 = squared_exp(x, x1, sq1) + jnp.where(tile == 1, NUGGET, 0.0) * eye
        l1 = nt3(split(k1 - nt3(split(l0), l10s)), h1s)
        l1 = jnp.where((tile > 1) | (lower & (tile == 1)), l1, 0.0)
        return l0, l1

    @pl.loop(0, tile_cols)
    def _(c2):
        l0, l1 = panels_of(colp[c2], c2 * cols_n + col_id)
        lh[c2, :, :size], ll[c2, :, :size] = split(l0)
        lh[c2, :, size:], ll[c2, :, size:] = split(l1)

    @pl.loop(0, tile_rows)
    def _(a):
        tile = a * rows_n + row_id
        x = pts[a]
        l0, l1 = panels_of(x, tile)
        lf[:, :size] = l0
        lf[:, size:] = l1
        ls = split(lf[...])
        rest = rhs[a] - nt3((yh[...], yl[...]), ls)
        solved[a] = jnp.where(tile == 0, y0, jnp.where(tile == 1, y1, rest))
        for c2 in range(tile_cols):
            tile_c = c2 * cols_n + col_id
            xc = colp[c2]
            k = squared_exp(x, xc, row_squares(xc)) + jnp.where(tile == tile_c, NUGGET, 0.0) * eye
            s = k - nt3(ls, (lh[c2], ll[c2]))
            s = jnp.where(tile >= PANELS, s, 0.0)
            if c2 == 0:
                s = jnp.where(tile_c == 0, lf[:, :size], jnp.where(tile_c == 1, lf[:, size:], s))
            for half in range(size // 128):
                out[a, pl.ds(c2 * (size // 128) + half, size, stride=tile_cols * size // 128), :] = s[
                    :, half * 128 : half * 128 + 128
                ]


def per_device(points, rhs):
    rows_n = lax.axis_size("row")
    cols_n = lax.axis_size("col")
    tile_rows, _, size, feat = points.shape
    width = rhs.shape[-1]
    tile_cols = tile_rows * rows_n // cols_n
    pts = points[:, 0]
    right = rhs[:, 0].swapaxes(1, 2)
    jobs = 2 * PANELS + tile_cols
    any_spec = pl.BlockSpec(memory_space=pl.ANY)
    vmem = pl.BlockSpec(memory_space=pltpu.VMEM)
    piv, colp, rpiv = pl.pallas_call(
        functools.partial(fetch_kernel, rows_n, cols_n, tile_cols),
        out_shape=(
            jax.ShapeDtypeStruct((PANELS, size, feat), F32),
            jax.ShapeDtypeStruct((tile_cols, size, feat), F32),
            jax.ShapeDtypeStruct((PANELS, width, size), F32),
        ),
        in_specs=[any_spec] * 2,
        out_specs=(any_spec,) * 3,
        scratch_shapes=[
            pltpu.SemaphoreType.DMA((jobs, rows_n)),
            pltpu.SemaphoreType.DMA((jobs, 2)),
            pltpu.SemaphoreType.DMA((jobs,)),
        ],
        compiler_params=pltpu.CompilerParams(collective_id=0, has_side_effects=True),
        name="fetch",
    )(pts, right)
    factored, solved = pl.pallas_call(
        functools.partial(main_kernel, rows_n, cols_n),
        out_shape=(
            jax.ShapeDtypeStruct((tile_rows, size * tile_cols * size // 128, 128), F32),
            jax.ShapeDtypeStruct((tile_rows, width, size), F32),
        ),
        in_specs=[any_spec] * 5,
        out_specs=(vmem,) * 2,
        scratch_shapes=[
            pltpu.VMEM(pts.shape, F32),
            pltpu.VMEM(piv.shape, F32),
            pltpu.VMEM(colp.shape, F32),
            pltpu.VMEM(right.shape, F32),
            pltpu.VMEM(rpiv.shape, F32),
            pltpu.SemaphoreType.DMA((5,)),
            pltpu.VMEM((NB, 2 * NB), F32),
            pltpu.VMEM((size, 2 * size), F32),
            pltpu.VMEM((size, size), F32),
            pltpu.VMEM((size, size), F32),
            pltpu.VMEM((size, size), F32),
            pltpu.VMEM((size, 2 * size), F32),
            pltpu.VMEM((tile_cols, size, 2 * size), BF16),
            pltpu.VMEM((tile_cols, size, 2 * size), BF16),
            pltpu.VMEM((width, 2 * size), BF16),
            pltpu.VMEM((width, 2 * size), BF16),
        ],
        compiler_params=pltpu.CompilerParams(vmem_limit_bytes=48 * 1024 * 1024),
        name="panels",
    )(pts, piv, colp, right, rpiv)
    factored = factored.reshape(tile_rows, 1, size, tile_cols, 1, size)
    return factored, solved.swapaxes(1, 2)[:, None]


def solution(mesh):
    return jax.shard_map(
        per_device,
        mesh=mesh,
        in_specs=(P(None, "row", None, None), P(None, "row", None, "col")),
        out_specs=(P(None, "row", None, None, "col", None), P(None, "row", None, "col")),
        check_vma=False,
    )
```

```python
import functools

import jax
import jax.numpy as jnp
from jax import lax
from jax.experimental import pallas as pl
from jax.experimental.pallas import tpu as pltpu
from jax.sharding import PartitionSpec as P

PANELS = 2
SCALE = 3.0
NUGGET = 1.0
HIGHEST = lax.Precision.HIGHEST
MESH = pl.DeviceIdType.MESH
F32 = jnp.float32
BF16 = jnp.bfloat16
NB = 128


def fetch_kernel(rows_n, cols_n, tile_cols, pts, prhs, piv, colp, rpiv, send, recv, local):
    row_id = lax.axis_index("row")
    col_id = lax.axis_index("col")
    stride = cols_n // rows_n

    barrier = pltpu.get_barrier_semaphore()
    for step in range(1, rows_n):
        other = lax.rem(row_id + step, rows_n)
        pl.semaphore_signal(barrier, inc=1, device_id={"row": other}, device_id_type=MESH)
    pl.semaphore_wait(barrier, rows_n - 1)

    jobs = []
    for k in range(PANELS):
        jobs.append((k % rows_n, pts.at[k // rows_n], piv.at[k]))
        jobs.append((k % rows_n, prhs.at[k // rows_n], rpiv.at[k]))
    for c2 in range(tile_cols):
        slot = c2 * stride + col_id // rows_n
        jobs.append((lax.rem(col_id, rows_n), pts.at[slot], colp.at[c2]))

    chips = rows_n // 2
    chip, core = row_id // 2, lax.rem(row_id, 2)
    sibling = row_id + 1 - 2 * core

    def half_of(ref, half):
        height = ref.shape[0] // 2
        return ref.at[pl.ds(pl.multiple_of(half * height, height), height)]

    def remote(number, half, dest, slot, relay=False):
        _, src, dst = jobs[number]
        return pltpu.make_async_remote_copy(
            src_ref=half_of(dst if relay else src, half),
            dst_ref=half_of(dst, half),
            send_sem=send.at[number, slot],
            recv_sem=recv.at[number, half],
            device_id={"row": dest},
            device_id_type=MESH,
        )

    def sends(number):
        out = []
        for step in range(1, chips):
            for half in range(2):
                dest = 2 * lax.rem(chip + step, chips) + half
                out.append(remote(number, half, dest, 2 * step + half))
        return out + [remote(number, half, sibling, half) for half in range(2)]

    for number, (owner, src, dst) in enumerate(jobs):

        @pl.when(row_id == owner)
        def _(number=number, src=src, dst=dst):
            for copy in sends(number):
                copy.start()
            pltpu.make_async_copy(src, dst, local.at[number]).start()

    for number, (owner, src, dst) in enumerate(jobs):

        @pl.when(chip != owner // 2)
        def _(number=number):
            relay = remote(number, core, sibling, 0, relay=True)
            relay.wait_recv()
            relay.start()

    for number, (owner, src, dst) in enumerate(jobs):

        @pl.when(row_id == owner)
        def _(number=number, src=src, dst=dst):
            for copy in sends(number):
                copy.wait_send()
            pltpu.make_async_copy(src, dst, local.at[number]).wait()

        @pl.when(sibling == owner)
        def _(number=number):
            for half in range(2):
                remote(number, half, sibling, half).wait_recv()

        @pl.when(chip != owner // 2)
        def _(number=number):
            remote(number, core, sibling, 0, relay=True).wait_send()
            remote(number, 1 - core, sibling, 0, relay=True).wait_recv()


def split(x):
    hi = x.astype(BF16)
    return hi, (x - hi.astype(F32)).astype(BF16)


def nt(a, b):
    return lax.dot_general(a, b, (((1,), (1,)), ((), ())), preferred_element_type=F32)


def nt3(a, b):
    return nt(a[0], b[0]) + (nt(a[0], b[1]) + nt(a[1], b[0]))


def squared_exp(a, b, b_sq):
    a_sq = jnp.sum(a * a, axis=1, keepdims=True)
    inner = nt3(split(a), split(b))
    return jnp.exp((-SCALE / a.shape[1]) * (a_sq + b_sq - 2.0 * inner))


def row_squares(b):
    ones = jnp.ones((8, b.shape[1]), F32)
    return lax.dot_general(
        ones, b * b, (((1,), (1,)), ((), ())), precision=HIGHEST, preferred_element_type=F32
    )[:1]


def spread(column):
    return jnp.broadcast_to(column, (column.shape[0], 2 * NB))


def base_inverse(block, base):
    eye = (
        lax.broadcasted_iota(jnp.int32, (NB, NB), 0) == lax.broadcasted_iota(jnp.int32, (NB, NB), 1)
    ).astype(F32)
    wide = jnp.concatenate([block, eye], axis=1)
    v = [wide[8 * q : 8 * q + 8] for q in range(NB // 8)]
    for j in range(0, NB, 2):
        q0, s = divmod(j, 8)
        first = [spread(v[q][:, j : j + 1]) for q in range(q0, NB // 8)]
        second = [spread(v[q][:, j + 1 : j + 2]) for q in range(q0, NB // 8)]
        r0, r1 = v[q0][s : s + 1], v[q0][s + 1 : s + 2]
        a, b = first[0][s : s + 1], second[0][s : s + 1]
        b1, c = first[0][s + 1 : s + 2], second[0][s + 1 : s + 2]
        det = a * c - b * b1
        inv_det = 1.0 / det
        e1 = a * r1 - b1 * r0
        s0 = (c * r0 - b * r1) * inv_det
        s1 = e1 * inv_det
        rs = lax.rsqrt(a)
        base[j : j + 1, :] = r0 * rs
        base[j + 1 : j + 2, :] = e1 * (lax.rsqrt(det) * rs)
        for q in range(q0 if s < 6 else q0 + 1, NB // 8):
            v[q] = v[q] - first[q - q0] * s0 - second[q - q0] * s1
    return base[:, NB:]


def inverse_factor(w, h, base):
    size = h.shape[0]
    for j0 in range(0, size, NB):
        j1 = j0 + NB
        inv = base_inverse(w[j0:j1, j0:j1], base)
        rows = jnp.dot(inv, w[j0:j1, :], precision=HIGHEST, preferred_element_type=F32)
        h[j0:j1, :] = rows[:, size:]
        if j1 < size:
            panel = lax.dot_general(
                w[j1:, j0:j1], inv, (((1,), (1,)), ((), ())), precision=HIGHEST, preferred_element_type=F32
            )
            w[j1:, :] = w[j1:, :] - jnp.dot(
                panel, rows, precision=HIGHEST, preferred_element_type=F32
            )


def main_kernel(
    rows_n, cols_n, hpts, hpiv, hcolp, hrhs, hrpiv, out, solved,
    pts, piv, colp, rhs, rpiv, sems, base, w, h0, h1, l10, lf, lh, ll, yh, yl,
):
    copies = [
        pltpu.make_async_copy(src, dst, sems.at[n])
        for n, (src, dst) in enumerate(
            ((hpiv, piv), (hrpiv, rpiv), (hcolp, colp), (hpts, pts), (hrhs, rhs))
        )
    ]
    for copy in copies:
        copy.start()
    copies[0].wait()
    row_id = lax.axis_index("row")
    col_id = lax.axis_index("col")
    tile_rows, size, _ = pts.shape
    tile_cols = colp.shape[0]
    row_in = lax.broadcasted_iota(jnp.int32, (size, size), 0)
    col_in = lax.broadcasted_iota(jnp.int32, (size, size), 1)
    eye = (row_in == col_in).astype(F32)
    lower = row_in >= col_in
    x0, x1 = piv[0], piv[1]
    sq0, sq1 = row_squares(x0), row_squares(x1)

    w[:, :size] = squared_exp(x0, x0, sq0) + NUGGET * eye
    w[:, size:] = eye
    inverse_factor(w, h0, base)
    h0s = split(h0[...])
    l10[...] = nt3(split(squared_exp(x1, x0, sq0)), h0s)
    l10s = split(l10[...])
    w[:, :size] = squared_exp(x1, x1, sq1) + NUGGET * eye - nt3(l10s, l10s)
    w[:, size:] = eye
    inverse_factor(w, h1, base)
    h1s = split(h1[...])

    for copy in copies[1:]:
        copy.wait()
    y0 = nt3(split(rpiv[0]), h0s)
    y1 = nt3(split(rpiv[1] - nt3(split(y0), l10s)), h1s)
    yh[:, :size], yl[:, :size] = split(y0)
    yh[:, size:], yl[:, size:] = split(y1)

    def panels_of(x, tile):
        k0 = squared_exp(x, x0, sq0) + jnp.where(tile == 0, NUGGET, 0.0) * eye
        l0 = nt3(split(k0), h0s)
        l0 = jnp.where((tile != 0) | lower, l0, 0.0)
        k1 = squared_exp(x, x1, sq1) + jnp.where(tile == 1, NUGGET, 0.0) * eye
        l1 = nt3(split(k1 - nt3(split(l0), l10s)), h1s)
        l1 = jnp.where((tile > 1) | (lower & (tile == 1)), l1, 0.0)
        return l0, l1

    @pl.loop(0, tile_cols)
    def _(c2):
        l0, l1 = panels_of(colp[c2], c2 * cols_n + col_id)
        lh[c2, :, :size], ll[c2, :, :size] = split(l0)
        lh[c2, :, size:], ll[c2, :, size:] = split(l1)

    @pl.loop(0, tile_rows)
    def _(a):
        tile = a * rows_n + row_id
        x = pts[a]
        l0, l1 = panels_of(x, tile)
        lf[:, :size] = l0
        lf[:, size:] = l1
        ls = split(lf[...])
        rest = rhs[a] - nt3((yh[...], yl[...]), ls)
        solved[a] = jnp.where(tile == 0, y0, jnp.where(tile == 1, y1, rest))
        for c2 in range(tile_cols):
            tile_c = c2 * cols_n + col_id
            xc = colp[c2]
            k = squared_exp(x, xc, row_squares(xc)) + jnp.where(tile == tile_c, NUGGET, 0.0) * eye
            s = k - nt3(ls, (lh[c2], ll[c2]))
            s = jnp.where(tile >= PANELS, s, 0.0)
            if c2 == 0:
                s = jnp.where(tile_c == 0, lf[:, :size], jnp.where(tile_c == 1, lf[:, size:], s))
            for half in range(size // 128):
                out[a, pl.ds(c2 * (size // 128) + half, size, stride=tile_cols * size // 128), :] = s[
                    :, half * 128 : half * 128 + 128
                ]


def per_device(points, rhs):
    rows_n = lax.axis_size("row")
    cols_n = lax.axis_size("col")
    tile_rows, _, size, feat = points.shape
    width = rhs.shape[-1]
    tile_cols = tile_rows * rows_n // cols_n
    pts = points[:, 0]
    right = rhs[:, 0].swapaxes(1, 2)
    jobs = 2 * PANELS + tile_cols
    any_spec = pl.BlockSpec(memory_space=pl.ANY)
    vmem = pl.BlockSpec(memory_space=pltpu.VMEM)
    piv, colp, rpiv = pl.pallas_call(
        functools.partial(fetch_kernel, rows_n, cols_n, tile_cols),
        out_shape=(
            jax.ShapeDtypeStruct((PANELS, size, feat), F32),
            jax.ShapeDtypeStruct((tile_cols, size, feat), F32),
            jax.ShapeDtypeStruct((PANELS, width, size), F32),
        ),
        in_specs=[any_spec] * 2,
        out_specs=(any_spec,) * 3,
        scratch_shapes=[
            pltpu.SemaphoreType.DMA((jobs, rows_n)),
            pltpu.SemaphoreType.DMA((jobs, 2)),
            pltpu.SemaphoreType.DMA((jobs,)),
        ],
        compiler_params=pltpu.CompilerParams(collective_id=0, has_side_effects=True),
        name="fetch",
    )(pts, right)
    factored, solved = pl.pallas_call(
        functools.partial(main_kernel, rows_n, cols_n),
        out_shape=(
            jax.ShapeDtypeStruct((tile_rows, size * tile_cols * size // 128, 128), F32),
            jax.ShapeDtypeStruct((tile_rows, width, size), F32),
        ),
        in_specs=[pl.BlockSpec(memory_space=pltpu.HBM)] * 5,
        out_specs=(vmem,) * 2,
        scratch_shapes=[
            pltpu.VMEM(pts.shape, F32),
            pltpu.VMEM(piv.shape, F32),
            pltpu.VMEM(colp.shape, F32),
            pltpu.VMEM(right.shape, F32),
            pltpu.VMEM(rpiv.shape, F32),
            pltpu.SemaphoreType.DMA((5,)),
            pltpu.VMEM((NB, 2 * NB), F32),
            pltpu.VMEM((size, 2 * size), F32),
            pltpu.VMEM((size, size), F32),
            pltpu.VMEM((size, size), F32),
            pltpu.VMEM((size, size), F32),
            pltpu.VMEM((size, 2 * size), F32),
            pltpu.VMEM((tile_cols, size, 2 * size), BF16),
            pltpu.VMEM((tile_cols, size, 2 * size), BF16),
            pltpu.VMEM((width, 2 * size), BF16),
            pltpu.VMEM((width, 2 * size), BF16),
        ],
        compiler_params=pltpu.CompilerParams(vmem_limit_bytes=48 * 1024 * 1024),
        name="panels",
    )(pts, piv, colp, right, rpiv)
    factored = factored.reshape(tile_rows, 1, size, tile_cols, 1, size)
    return factored, solved.swapaxes(1, 2)[:, None]


def solution(mesh):
    return jax.shard_map(
        per_device,
        mesh=mesh,
        in_specs=(P(None, "row", None, None), P(None, "row", None, "col")),
        out_specs=(P(None, "row", None, None, "col", None), P(None, "row", None, "col")),
        check_vma=False,
    )
```

```python
import functools

import jax
import jax.numpy as jnp
from jax import lax
from jax.experimental import pallas as pl
from jax.experimental.pallas import tpu as pltpu
from jax.sharding import PartitionSpec as P

PANELS = 2
SCALE = 3.0
NUGGET = 1.0
HIGHEST = lax.Precision.HIGHEST
MESH = pl.DeviceIdType.MESH
F32 = jnp.float32
BF16 = jnp.bfloat16
NB = 128


def fetch_kernel(rows_n, cols_n, tile_cols, pts, prhs, piv, colp, rpiv, send, recv, local):
    row_id = lax.axis_index("row")
    col_id = lax.axis_index("col")
    stride = cols_n // rows_n

    barrier = pltpu.get_barrier_semaphore()
    for step in range(1, rows_n):
        other = lax.rem(row_id + step, rows_n)
        pl.semaphore_signal(barrier, inc=1, device_id={"row": other}, device_id_type=MESH)
    pl.semaphore_wait(barrier, rows_n - 1)

    jobs = []
    for k in range(PANELS):
        jobs.append((k % rows_n, pts.at[k // rows_n], piv.at[k]))
        jobs.append((k % rows_n, prhs.at[k // rows_n], rpiv.at[k]))
    for c2 in range(tile_cols):
        slot = c2 * stride + col_id // rows_n
        jobs.append((lax.rem(col_id, rows_n), pts.at[slot], colp.at[c2]))

    chips = rows_n // 2
    chip, core = row_id // 2, lax.rem(row_id, 2)
    sibling = row_id + 1 - 2 * core

    def half_of(ref, half):
        height = ref.shape[0] // 2
        return ref.at[pl.ds(pl.multiple_of(half * height, height), height)]

    def remote(number, half, dest, slot, relay=False):
        _, src, dst = jobs[number]
        return pltpu.make_async_remote_copy(
            src_ref=half_of(dst if relay else src, half),
            dst_ref=half_of(dst, half),
            send_sem=send.at[number, slot],
            recv_sem=recv.at[number, half],
            device_id={"row": dest},
            device_id_type=MESH,
        )

    def sends(number):
        out = []
        for step in range(1, chips):
            for half in range(2):
                dest = 2 * lax.rem(chip + step, chips) + half
                out.append(remote(number, half, dest, 2 * step + half))
        return out + [remote(number, half, sibling, half) for half in range(2)]

    for number, (owner, src, dst) in enumerate(jobs):

        @pl.when(row_id == owner)
        def _(number=number, src=src, dst=dst):
            for copy in sends(number):
                copy.start()
            pltpu.make_async_copy(src, dst, local.at[number]).start()

    for number, (owner, src, dst) in enumerate(jobs):

        @pl.when(chip != owner // 2)
        def _(number=number):
            relay = remote(number, core, sibling, 0, relay=True)
            relay.wait_recv()
            relay.start()

    for number, (owner, src, dst) in enumerate(jobs):

        @pl.when(row_id == owner)
        def _(number=number, src=src, dst=dst):
            for copy in sends(number):
                copy.wait_send()
            pltpu.make_async_copy(src, dst, local.at[number]).wait()

        @pl.when(sibling == owner)
        def _(number=number):
            for half in range(2):
                remote(number, half, sibling, half).wait_recv()

        @pl.when(chip != owner // 2)
        def _(number=number):
            remote(number, core, sibling, 0, relay=True).wait_send()
            remote(number, 1 - core, sibling, 0, relay=True).wait_recv()


def split(x):
    hi = x.astype(BF16)
    return hi, (x - hi.astype(F32)).astype(BF16)


def nt(a, b):
    return lax.dot_general(a, b, (((1,), (1,)), ((), ())), preferred_element_type=F32)


def nt3(a, b):
    return nt(a[0], b[0]) + (nt(a[0], b[1]) + nt(a[1], b[0]))


def squared_exp(a, b, b_sq):
    a_sq = jnp.sum(a * a, axis=1, keepdims=True)
    inner = nt3(split(a), split(b))
    return jnp.exp((-SCALE / a.shape[1]) * (a_sq + b_sq - 2.0 * inner))


def row_squares(b):
    ones = jnp.ones((8, b.shape[1]), F32)
    return lax.dot_general(
        ones, b * b, (((1,), (1,)), ((), ())), precision=HIGHEST, preferred_element_type=F32
    )[:1]


def spread(column):
    return jnp.broadcast_to(column, (column.shape[0], 2 * NB))


def base_inverse(block, base):
    eye = (
        lax.broadcasted_iota(jnp.int32, (NB, NB), 0) == lax.broadcasted_iota(jnp.int32, (NB, NB), 1)
    ).astype(F32)
    wide = jnp.concatenate([block, eye], axis=1)
    v = [wide[8 * q : 8 * q + 8] for q in range(NB // 8)]
    for j in range(0, NB, 4):
        q0, s = divmod(j, 8)
        cols = [[spread(v[q][:, j + n : j + n + 1]) for n in range(4)] for q in range(q0, NB // 8)]
        rows = [v[q0][s + n : s + n + 1] for n in range(4)]
        at = [[cols[0][n][s + m : s + m + 1] for n in range(4)] for m in range(4)]

        def pair(r0, r1, a, b, b1, c, where):
            det = a * c - b * b1
            inv_det = 1.0 / det
            e1 = a * r1 - b1 * r0
            rs = lax.rsqrt(a)
            base[where : where + 1, :] = r0 * rs
            base[where + 1 : where + 2, :] = e1 * (lax.rsqrt(det) * rs)
            return a, b, b1, c, inv_det, (c * r0 - b * r1) * inv_det, e1 * inv_det

        a, b, b1, c, inv_det, s0, s1 = pair(
            rows[0], rows[1], at[0][0], at[0][1], at[1][0], at[1][1], j
        )
        u0 = [(c * at[0][n] - b * at[1][n]) * inv_det for n in (2, 3)]
        u1 = [(a * at[1][n] - b1 * at[0][n]) * inv_det for n in (2, 3)]
        r2, r3 = (rows[m] - at[m][0] * s0 - at[m][1] * s1 for m in (2, 3))
        p = [[at[m][n + 2] - at[m][0] * u0[n] - at[m][1] * u1[n] for n in (0, 1)] for m in (2, 3)]
        s2, s3 = pair(r2, r3, p[0][0], p[0][1], p[1][0], p[1][1], j + 2)[5:]
        for q in range(q0 if s == 0 else q0 + 1, NB // 8):
            k0, k1, k2, k3 = cols[q - q0]
            k2 = k2 - k0 * u0[0] - k1 * u1[0]
            k3 = k3 - k0 * u0[1] - k1 * u1[1]
            v[q] = v[q] - k0 * s0 - k1 * s1 - k2 * s2 - k3 * s3
    return base[:, NB:]


def inverse_factor(w, h, base):
    size = h.shape[0]
    for j0 in range(0, size, NB):
        j1 = j0 + NB
        inv = base_inverse(w[j0:j1, j0:j1], base)
        rows = jnp.dot(inv, w[j0:j1, :], precision=HIGHEST, preferred_element_type=F32)
        h[j0:j1, :] = rows[:, size:]
        if j1 < size:
            panel = lax.dot_general(
                w[j1:, j0:j1], inv, (((1,), (1,)), ((), ())), precision=HIGHEST, preferred_element_type=F32
            )
            w[j1:, :] = w[j1:, :] - jnp.dot(
                panel, rows, precision=HIGHEST, preferred_element_type=F32
            )


def main_kernel(
    rows_n, cols_n, hpts, hpiv, hcolp, hrhs, hrpiv, out, solved,
    pts, piv, colp, rhs, rpiv, sems, base, w, h0, h1, l10, lf, lh, ll, yh, yl,
):
    copies = [
        pltpu.make_async_copy(src, dst, sems.at[n])
        for n, (src, dst) in enumerate(
            ((hpiv, piv), (hrpiv, rpiv), (hcolp, colp), (hpts, pts), (hrhs, rhs))
        )
    ]
    for copy in copies:
        copy.start()
    copies[0].wait()
    row_id = lax.axis_index("row")
    col_id = lax.axis_index("col")
    tile_rows, size, _ = pts.shape
    tile_cols = colp.shape[0]
    row_in = lax.broadcasted_iota(jnp.int32, (size, size), 0)
    col_in = lax.broadcasted_iota(jnp.int32, (size, size), 1)
    eye = (row_in == col_in).astype(F32)
    lower = row_in >= col_in
    x0, x1 = piv[0], piv[1]
    sq0, sq1 = row_squares(x0), row_squares(x1)

    w[:, :size] = squared_exp(x0, x0, sq0) + NUGGET * eye
    w[:, size:] = eye
    inverse_factor(w, h0, base)
    h0s = split(h0[...])
    l10[...] = nt3(split(squared_exp(x1, x0, sq0)), h0s)
    l10s = split(l10[...])
    w[:, :size] = squared_exp(x1, x1, sq1) + NUGGET * eye - nt3(l10s, l10s)
    w[:, size:] = eye
    inverse_factor(w, h1, base)
    h1s = split(h1[...])

    for copy in copies[1:]:
        copy.wait()
    y0 = nt3(split(rpiv[0]), h0s)
    y1 = nt3(split(rpiv[1] - nt3(split(y0), l10s)), h1s)
    yh[:, :size], yl[:, :size] = split(y0)
    yh[:, size:], yl[:, size:] = split(y1)

    def panels_of(x, tile):
        k0 = squared_exp(x, x0, sq0) + jnp.where(tile == 0, NUGGET, 0.0) * eye
        l0 = nt3(split(k0), h0s)
        l0 = jnp.where((tile != 0) | lower, l0, 0.0)
        k1 = squared_exp(x, x1, sq1) + jnp.where(tile == 1, NUGGET, 0.0) * eye
        l1 = nt3(split(k1 - nt3(split(l0), l10s)), h1s)
        l1 = jnp.where((tile > 1) | (lower & (tile == 1)), l1, 0.0)
        return l0, l1

    @pl.loop(0, tile_cols)
    def _(c2):
        l0, l1 = panels_of(colp[c2], c2 * cols_n + col_id)
        lh[c2, :, :size], ll[c2, :, :size] = split(l0)
        lh[c2, :, size:], ll[c2, :, size:] = split(l1)

    @pl.loop(0, tile_rows)
    def _(a):
        tile = a * rows_n + row_id
        x = pts[a]
        l0, l1 = panels_of(x, tile)
        lf[:, :size] = l0
        lf[:, size:] = l1
        ls = split(lf[...])
        rest = rhs[a] - nt3((yh[...], yl[...]), ls)
        solved[a] = jnp.where(tile == 0, y0, jnp.where(tile == 1, y1, rest))
        for c2 in range(tile_cols):
            tile_c = c2 * cols_n + col_id
            xc = colp[c2]
            k = squared_exp(x, xc, row_squares(xc)) + jnp.where(tile == tile_c, NUGGET, 0.0) * eye
            s = k - nt3(ls, (lh[c2], ll[c2]))
            s = jnp.where(tile >= PANELS, s, 0.0)
            if c2 == 0:
                s = jnp.where(tile_c == 0, lf[:, :size], jnp.where(tile_c == 1, lf[:, size:], s))
            for half in range(size // 128):
                out[a, pl.ds(c2 * (size // 128) + half, size, stride=tile_cols * size // 128), :] = s[
                    :, half * 128 : half * 128 + 128
                ]


def per_device(points, rhs):
    rows_n = lax.axis_size("row")
    cols_n = lax.axis_size("col")
    tile_rows, _, size, feat = points.shape
    width = rhs.shape[-1]
    tile_cols = tile_rows * rows_n // cols_n
    pts = points[:, 0]
    right = rhs[:, 0].swapaxes(1, 2)
    jobs = 2 * PANELS + tile_cols
    any_spec = pl.BlockSpec(memory_space=pl.ANY)
    vmem = pl.BlockSpec(memory_space=pltpu.VMEM)
    piv, colp, rpiv = pl.pallas_call(
        functools.partial(fetch_kernel, rows_n, cols_n, tile_cols),
        out_shape=(
            jax.ShapeDtypeStruct((PANELS, size, feat), F32),
            jax.ShapeDtypeStruct((tile_cols, size, feat), F32),
            jax.ShapeDtypeStruct((PANELS, width, size), F32),
        ),
        in_specs=[any_spec] * 2,
        out_specs=(any_spec,) * 3,
        scratch_shapes=[
            pltpu.SemaphoreType.DMA((jobs, rows_n)),
            pltpu.SemaphoreType.DMA((jobs, 2)),
            pltpu.SemaphoreType.DMA((jobs,)),
        ],
        compiler_params=pltpu.CompilerParams(collective_id=0, has_side_effects=True),
        name="fetch",
    )(pts, right)
    factored, solved = pl.pallas_call(
        functools.partial(main_kernel, rows_n, cols_n),
        out_shape=(
            jax.ShapeDtypeStruct((tile_rows, size * tile_cols * size // 128, 128), F32),
            jax.ShapeDtypeStruct((tile_rows, width, size), F32),
        ),
        in_specs=[pl.BlockSpec(memory_space=pltpu.HBM)] * 5,
        out_specs=(vmem,) * 2,
        scratch_shapes=[
            pltpu.VMEM(pts.shape, F32),
            pltpu.VMEM(piv.shape, F32),
            pltpu.VMEM(colp.shape, F32),
            pltpu.VMEM(right.shape, F32),
            pltpu.VMEM(rpiv.shape, F32),
            pltpu.SemaphoreType.DMA((5,)),
            pltpu.VMEM((NB, 2 * NB), F32),
            pltpu.VMEM((size, 2 * size), F32),
            pltpu.VMEM((size, size), F32),
            pltpu.VMEM((size, size), F32),
            pltpu.VMEM((size, size), F32),
            pltpu.VMEM((size, 2 * size), F32),
            pltpu.VMEM((tile_cols, size, 2 * size), BF16),
            pltpu.VMEM((tile_cols, size, 2 * size), BF16),
            pltpu.VMEM((width, 2 * size), BF16),
            pltpu.VMEM((width, 2 * size), BF16),
        ],
        compiler_params=pltpu.CompilerParams(vmem_limit_bytes=62 * 1024 * 1024),
        name="panels",
    )(pts, piv, colp, right, rpiv)
    factored = factored.reshape(tile_rows, 1, size, tile_cols, 1, size)
    return factored, solved.swapaxes(1, 2)[:, None]


def solution(mesh):
    return jax.shard_map(
        per_device,
        mesh=mesh,
        in_specs=(P(None, "row", None, None), P(None, "row", None, "col")),
        out_specs=(P(None, "row", None, None, "col", None), P(None, "row", None, "col")),
        check_vma=False,
    )
```
